512 devices in a mesh: src: 16 (over x, y_hi), snk: 32 (over z, y_lo, core).
Axes of the slice: x: 4, y: 8 (y_hi: 4, y_lo: 2; y = y_hi * 2 + y_lo), z: 8, core: 2. Of those that a mesh axis runs over, the one named last changes fastest.
Arguments:
- perambulator: bfloat16 [128, 32, 256, 512], P('snk', 'src'), may hold values from -0.25 to 0.25
- sink_elemental: bfloat16 [128, 256, 512], P('snk', 'src'), may hold values from -0.25 to 0.25
- source_elemental: bfloat16 [32, 256, 512], P('src', 'snk'), may hold values from -0.25 to 0.25
Outputs:
- correlator: float32 [4, 32, 128], P(None, 'src', 'snk')
The draws below stay inside these ranges and needn't reach their ends.
All inputs are finite; a program needn't handle non-finite values.
Results may differ from the reference program's by a relative error of at most 0.0065.
Values may be sent and summed in bfloat16 or wider, within the bound.
A program may use at most 64 MiB of HBM per device.

```python
import jax
import jax.numpy as jnp
from jax import lax

NV = 256
DT = 1
NT = 128
NSRC = 32


def steps_of(own_key, extent, shards, least, largest):
    def one(dim, shards_of):
        heights = jax.random.uniform(jax.random.fold_in(jax.random.fold_in(own_key, 6), dim), (shards_of,), jnp.float32, least / len(shards), largest / len(shards))
        return jnp.repeat(jnp.exp(heights), extent[dim] // shards_of).reshape((-1,) + (1,) * (len(extent) - dim - 1))

    gain = one(*shards[0])
    for cut in shards[1:]:
        gain = gain * one(*cut)
    return gain


def centred(rng, shape, scale, most, pieces=(), dtype=jnp.bfloat16):
    level = steps_of(rng, shape, pieces, -0.22, 0.18) if pieces else 1.0
    entries = jax.random.normal(rng, shape, jnp.float32) * scale * level
    return jnp.minimum(jnp.maximum(entries, -most), most).astype(dtype)


def setup_inputs(seed: int = 0) -> dict:
    streams_of = jax.random.split(jax.random.key(seed), 4)
    return {
        "perambulator": centred(streams_of[0], (NT, NSRC, NV, 2 * NV), (2 * NV) ** -0.5, 0.25, ((0, 32), (1, 16))),
        "sink_elemental": centred(streams_of[1], (NT, NV, 2 * NV), (2 * NV) ** -0.5, 0.25, ((0, 32), (1, 16))),
        "source_elemental": centred(streams_of[2], (NSRC, NV, 2 * NV), (2 * NV) ** -0.5, 0.25, ((0, 16), (1, 32))),
    }


def complex_product(factor, second):
    order = second.shape[0]
    lower = jnp.concatenate([-second[:, order:], second[:, :order]], 1)
    stacked = jnp.concatenate([second, lower], 0)
    return jnp.dot(factor, stacked, preferred_element_type=jnp.float32)


def adjoint(matrix):
    order = matrix.shape[0]
    return jnp.concatenate([matrix[:, :order].T, -matrix[:, order:].T], 1)


def trace_adjoint(first, second):
    order = first.shape[0]
    first = first.astype(jnp.float32)
    second = second.astype(jnp.float32)
    real_part = jnp.sum(first[:, :order] * second[:, :order] + first[:, order:] * second[:, order:])
    imag_part = jnp.sum(first[:, order:] * second[:, :order] - first[:, :order] * second[:, order:])
    return real_part, imag_part


def make_first(sink_elem, tau_now, source_elem):
    head = complex_product(sink_elem, tau_now).astype(jnp.bfloat16)
    return complex_product(head, source_elem).astype(jnp.bfloat16)


def make_other(sink_elem, tau_now, source_elem):
    back = complex_product(adjoint(sink_elem), tau_now).astype(jnp.bfloat16)
    return complex_product(back, adjoint(source_elem)).astype(jnp.bfloat16)


def contract(first, tau_now, tau_next, other_next):
    swapped = complex_product(first, adjoint(tau_next)).astype(jnp.bfloat16)
    loop_product = complex_product(swapped, other_next)
    box_re, box_im = trace_adjoint(loop_product, tau_now)
    one_re, one_im = trace_adjoint(first, tau_now)
    two_re, two_im = trace_adjoint(other_next, tau_next)
    return jnp.stack([one_re * two_re - one_im * two_im, one_re * two_im + one_im * two_re, box_re, box_im])


def reference(perambulator, sink_elemental, source_elemental):
    def one_source(inputs):
        tau_source, source_elem = inputs
        firsts = jax.vmap(make_first, in_axes=(0, 0, None))(sink_elemental, tau_source, source_elem)
        others = jax.vmap(make_other, in_axes=(0, 0, None))(sink_elemental, tau_source, source_elem)
        tau_shifted = jnp.roll(tau_source, -DT, axis=0)
        other_shifted = jnp.roll(others, -DT, axis=0)
        return jax.vmap(contract)(firsts, tau_source, tau_shifted, other_shifted)

    values = lax.map(one_source, (jnp.swapaxes(perambulator, 0, 1), source_elemental))
    return jnp.transpose(values, (2, 0, 1))
```

```python
import jax
import jax.numpy as jnp
from jax import lax
from jax.experimental import pallas as pl
from jax.experimental.pallas import tpu as pltpu
from jax.sharding import PartitionSpec as P

NX, NYH, NZ = 4, 4, 8
T, S, N = 4, 2, 256
W = 2 * N
ROWS = 16
BF, F32 = jnp.bfloat16, jnp.float32


def mm(a, b):
    return lax.dot_general(a, b, (((1,), (0,)), ((), ())), preferred_element_type=F32)


def mm_nt(a, b):
    return lax.dot_general(a, b, (((1,), (1,)), ((), ())), preferred_element_type=F32)


def trace_adjoint(pr, pi, qr, qi):
    pr, pi, qr, qi = (v.astype(F32) for v in (pr, pi, qr, qi))
    return jnp.sum(pr * qr + pi * qi), jnp.sum(pi * qr - pr * qi)


def halves(m):
    return m[:, :N], m[:, N:]


def upright(m):
    return jnp.concatenate([m[:, :N], m[:, N:]], axis=0)


def lower_rows(m):
    return jnp.concatenate([-m[:, N:], m[:, :N]], axis=1)


def kernel(
    tau, sink, slab, out,
    tbig, tadj, tlast, abuf, bslab, edge, gbuf, bbig, bleft, badj, ubig, vbig, dre, dim,
    tau_sem, own_sem, y_send, y_recv, x_send, x_recv, f_send, f_recv,
    l_send, l_recv, z_send, z_recv, c_send, c_recv, e_send, e_recv,
):
    j, k = lax.axis_index("src"), lax.axis_index("snk")
    x, yh = j // NYH, j % NYH
    c, q = k % 2, k // 2
    yl, z = q % 2, q // 2

    def at(xx, yy):
        return (lax.rem(xx + NX, NX) * NYH + lax.rem(yy + NYH, NYH), k)

    def along_z(d):
        return (j, lax.rem(z + d, NZ) * 4 + yl * 2 + c)

    before = (j, lax.rem(k + 4 * NZ - 1, 4 * NZ))
    after = (j, lax.rem(k + 1, 4 * NZ))
    other_core = (j, k + 1 - 2 * c)
    other_y = (j, k + 2 - 4 * yl)

    def remote(src, dst, send, recv, device):
        return pltpu.make_async_remote_copy(
            src_ref=src, dst_ref=dst, send_sem=send, recv_sem=recv,
            device_id=device, device_id_type=pl.DeviceIdType.MESH,
        )

    loads = {}
    for t in range(T):
        for s in range(S):
            into = tbig.at[t, s, pl.ds(0, N)] if t < T - 1 else tlast.at[s]
            loads[t, s] = pltpu.make_async_copy(tau.at[t, s], into, tau_sem.at[t, s])
            loads[t, s].start()
    mine = pl.ds(pl.multiple_of(64 * x + ROWS * yh, ROWS), ROWS)
    owns = [pltpu.make_async_copy(sink.at[t], abuf.at[t, mine], own_sem.at[t]) for t in range(T)]
    owns.append(pltpu.make_async_copy(slab, bslab.at[c, q], own_sem.at[T]))
    for copy in owns:
        copy.start()

    barrier = pltpu.get_barrier_semaphore()
    peers = [at(x, yh + d) for d in range(1, NYH)] + [at(x + 1, yh), at(x - 1, yh)]
    peers += [before, after, other_y] + [along_z(d) for d in range(1, NZ)]
    for peer in peers:
        pl.semaphore_signal(barrier, inc=1, device_id=peer, device_id_type=pl.DeviceIdType.MESH)
    pl.semaphore_wait(barrier, len(peers))

    ys, xs, fs = {}, {}, {}
    started = []

    def go(copy):
        copy.start()
        started.append(copy)
        return copy

    ylo = go(remote(slab, bslab.at[c, q], l_send, l_recv, other_y))
    for t in range(T):
        for d in range(1, NYH):
            ys[t, d] = go(remote(
                sink.at[t], abuf.at[t, mine], y_send.at[t, d - 1], y_recv.at[t, d - 1], at(x, yh + d)
            ))

    def block(xx, start=0, size=64):
        first = pl.multiple_of(64 * lax.rem(xx + NX, NX) + start, 32)
        return pl.ds(first, size)

    def to_x(t):
        owns[t].wait()
        for d in range(1, NYH):
            ys[t, d].wait_recv()
        for way, step in ((0, 1), (1, -1)):
            rows = abuf.at[t, block(x)]
            xs[t, way] = go(remote(rows, rows, x_send.at[t, way], x_recv.at[t, way], at(x + step, yh)))

    def forward(t):
        for way, step in ((0, 1), (1, -1)):
            xs[t, way].wait_recv()
            rows = abuf.at[t, block(x - step, 32 * way, 32)]
            fs[t, way] = go(remote(rows, rows, f_send.at[t, way], f_recv.at[t, way], at(x + step, yh)))

    def arrived(t):
        for way in range(2):
            fs[t, way].wait_recv()

    def per_source(body):
        lax.fori_loop(0, S, lambda s, carry: (body(s), carry)[1], 0)

    def prepare(t):
        for s in range(S):
            loads[t, s].wait()

        def body(s):
            m = tbig[t, s, :N]
            tbig[t, s, N:] = lower_rows(m)
            re, im = m[:, :N].T, m[:, N:].T
            tadj[t, s, :N, :N] = re
            tadj[t, s, :N, N:] = im
            tadj[t, s, N:, :N] = -im
            tadj[t, s, N:, N:] = re

        per_source(body)

    def sandwich(t):
        def body(s):
            head = mm(abuf[t], tbig[t, s]).astype(BF)
            g = mm(tadj[t, s], upright(head)).astype(BF)
            gbuf[t, s, :, :N] = g[:N]
            gbuf[t, s, :, N:] = g[N:]

        per_source(body)

    def one_trace(t, g, s):
        dre[t, s], dim[t, s] = trace_adjoint(*halves(g), *halves(badj[s]))

    def box_of(t):
        def body(s):
            left = mm(gbuf[t, s], bbig[s])
            right = mm(bleft[s], upright(gbuf[t + 1, s]))
            out[2, s, t], out[3, s, t] = trace_adjoint(*halves(left), right[:N], right[N:])

        per_source(body)

    prepare(0)
    to_x(0)
    ylo.wait_recv()
    owns[T].wait()
    zs = []
    two = bslab.at[c, pl.ds(2 * z, 2)]
    for d in range(1, NZ):
        zs.append(go(remote(two, two, z_send.at[d - 1], z_recv.at[d - 1], along_z(d))))
    prepare(1)
    to_x(1)
    forward(0)
    prepare(2)
    to_x(2)
    forward(1)
    arrived(0)
    sandwich(0)
    edges = [go(remote(gbuf.at[0, s], edge.at[s], e_send.at[s], e_recv.at[s], before)) for s in range(S)]
    to_x(3)
    forward(2)
    for copy in zs:
        copy.wait_recv()
    over = go(remote(bslab.at[c], bslab.at[c], c_send, c_recv, other_core))
    arrived(1)
    sandwich(1)
    forward(3)
    over.wait_recv()

    def spread(s):
        for n in range(16):
            first = bslab[0, n].astype(F32)
            second = bslab[1, n].astype(F32)
            low = jnp.where(s == 0, first[:8], first[8:])
            high = jnp.where(s == 0, second[:8], second[8:])
            bbig[s, pl.ds(ROWS * n, ROWS)] = jnp.concatenate([low, high], axis=0).astype(BF)
        m = bbig[s, :N]
        re, im = halves(m)
        bbig[s, N:] = lower_rows(m)
        bleft[s, :N, :N] = re
        bleft[s, :N, N:] = -im
        bleft[s, N:, :N] = im
        bleft[s, N:, N:] = re
        badj[s, :, :N] = re.T
        badj[s, :, N:] = -im.T

    per_source(spread)

    def outer(s):
        u = mm(tlast[s], bbig[s]).astype(BF)
        ubig[s, :N] = u
        ubig[s, N:] = lower_rows(u)
        v = mm_nt(tlast[s], bbig[s]).astype(BF)
        vbig[s, :N] = v
        vbig[s, N:] = lower_rows(v)

    for s in range(S):
        loads[T - 1, s].wait()
    per_source(outer)
    box_of(0)
    arrived(2)
    sandwich(2)
    box_of(1)

    def traces(s):
        for t in range(T - 1):
            one_trace(t, gbuf[t, s], s)

    per_source(traces)
    arrived(3)

    def last(s):
        a = halves(abuf[T - 1])
        dre[T - 1, s], dim[T - 1, s] = trace_adjoint(*a, *halves(mm_nt(tlast[s], ubig[s])))
        g = gbuf[T - 2, s]
        n = (mm(vbig[s, :N], jnp.concatenate([g, lower_rows(g)], axis=0))).astype(BF)
        out[2, s, T - 2], out[3, s, T - 2] = trace_adjoint(*halves(mm_nt(n, vbig[s])), *a)

    per_source(last)

    for copy in edges:
        copy.wait_recv()

    def final(s):
        a = halves(abuf[T - 1])
        g = edge[s]
        one_trace(T, g, s)
        n = mm(ubig[s, :N], jnp.concatenate([g, lower_rows(g)], axis=0)).astype(BF)
        out[2, s, T - 1], out[3, s, T - 1] = trace_adjoint(*a, *halves(mm_nt(n, ubig[s])))

    per_source(final)
    for s in range(S):
        for t in range(T):
            ar, ai, br, bi = dre[t, s], dim[t, s], dre[t + 1, s], dim[t + 1, s]
            out[0, s, t] = ar * br + ai * bi
            out[1, s, t] = ai * br - ar * bi
    for copy in started:
        copy.wait_send()


def shards(perambulator, sink_elemental, source_elemental):
    dma = pltpu.SemaphoreType.DMA
    vmem = pltpu.VMEM
    return pl.pallas_call(
        kernel,
        out_shape=jax.ShapeDtypeStruct((4, S, T), F32),
        in_specs=[pl.BlockSpec(memory_space=pl.ANY)] * 3,
        out_specs=pl.BlockSpec(memory_space=pltpu.SMEM),
        scratch_shapes=[
            vmem((T - 1, S, W, W), BF),
            vmem((T - 1, S, W, W), BF),
            vmem((S, N, W), BF),
            vmem((T, N, W), BF),
            vmem((2, 16, ROWS, W), BF),
            vmem((S, N, W), BF),
            vmem((T - 1, S, N, W), BF),
            vmem((S, W, W), BF),
            vmem((S, W, W), BF),
            vmem((S, N, W), BF),
            vmem((S, W, W), BF),
            vmem((S, W, W), BF),
            pltpu.SMEM((T + 1, S), F32),
            pltpu.SMEM((T + 1, S), F32),
            dma((T, S)),
            dma((T + 1,)),
            dma((T, NYH - 1)),
            dma((T, NYH - 1)),
            dma((T, 2)),
            dma((T, 2)),
            dma((T, 2)),
            dma((T, 2)),
            dma,
            dma,
            dma((NZ - 1,)),
            dma((NZ - 1,)),
            dma,
            dma,
            dma((S,)),
            dma((S,)),
        ],
        compiler_params=pltpu.CompilerParams(
            collective_id=0, has_side_effects=True, vmem_limit_bytes=48 * 1024 * 1024
        ),
        cost_estimate=pl.CostEstimate(flops=4_600_000_000, bytes_accessed=2_300_000, transcendentals=0),
    )(perambulator, sink_elemental, source_elemental.reshape(ROWS, W))


def solution(mesh):
    in_specs = (P("snk", "src", None, None), P("snk", "src", None), P("src", "snk", None))
    out_specs = P(None, "src", "snk")
    return jax.shard_map(shards, mesh=mesh, in_specs=in_specs, out_specs=out_specs, check_vma=False)
```

```python
import jax
import jax.numpy as jnp
from jax import lax
from jax.experimental import pallas as pl
from jax.experimental.pallas import tpu as pltpu
from jax.sharding import PartitionSpec as P

NX, NYH, NZ = 4, 4, 8
STEP = (1, -1)
LAST = 4 * NZ - 1
T, S, N = 4, 2, 256
GROUPS = ((0, 2), (2, 2), (4, 1))
W = 2 * N
ROWS = 16
BF, F32 = jnp.bfloat16, jnp.float32


def mm(a, b):
    return lax.dot_general(a, b, (((1,), (0,)), ((), ())), preferred_element_type=F32)


def mm_nt(a, b):
    return lax.dot_general(a, b, (((1,), (1,)), ((), ())), preferred_element_type=F32)


def trace_adjoint(pr, pi, qr, qi):
    pr, pi, qr, qi = (v.astype(F32) for v in (pr, pi, qr, qi))
    return jnp.sum(pr * qr + pi * qi), jnp.sum(pi * qr - pr * qi)


def halves(m):
    return m[:, :N], m[:, N:]


def lower_rows(m):
    return jnp.concatenate([-m[:, N:], m[:, :N]], axis=1)


def kernel(
    tau, sink, slab, out,
    tall, abig, bslab, bbig, ubig, vdag, xbig, zlast, dout, dnext, dre, dim,
    tau_sem, own_sem, y_send, y_recv, v_send, v_recv, x_send, x_recv, f_send, f_recv,
    l_send, l_recv, z_send, z_recv, h_send, h_recv, e_send, e_recv, wrap_sem,
):
    j, k = lax.axis_index("src"), lax.axis_index("snk")
    x, yh = j // NYH, j % NYH
    c, q = k % 2, k // 2
    yl, z = q % 2, q // 2
    near = q + 1 - 2 * yl

    def at(xx, yy):
        return (lax.rem(xx + NX, NX) * NYH + lax.rem(yy + NYH, NYH), k)

    def along_z(d):
        return (j, lax.rem(z + d + NZ, NZ) * 4 + yl * 2 + c)

    before = (j, lax.rem(k + 4 * NZ - 1, 4 * NZ))
    after = (j, lax.rem(k + 1, 4 * NZ))
    other_core = (j, k + 1 - 2 * c)
    other_y = (j, k + 2 - 4 * yl)

    barrier = pltpu.get_barrier_semaphore()
    peers = [at(x, yh + 1), at(x, yh - 1), at(x + 1, yh), at(x - 1, yh)]
    peers += [other_y, other_core]

    def tell(semaphore, device):
        pl.semaphore_signal(semaphore, inc=1, device_id=device, device_id_type=pl.DeviceIdType.MESH)

    for peer in peers:
        tell(barrier, peer)

    @pl.when((c == 1) & (k < LAST))
    def _():
        tell(barrier, after)

    @pl.when(k == 0)
    def _():
        tell(barrier, before)

    for i in range(1, NZ):

        @pl.when(z + i < NZ)
        def _():
            tell(barrier, along_z(i))

    def chunk(xx, yy):
        row = 64 * lax.rem(xx + NX, NX) + ROWS * lax.rem(yy + NYH, NYH)
        return pl.ds(pl.multiple_of(row, ROWS), ROWS)

    mine = chunk(x, yh)
    own = pltpu.make_async_copy(sink, abig.at[pl.ds(0, T), mine], own_sem.at[0])
    own_slab = pltpu.make_async_copy(slab, bslab.at[c, q], own_sem.at[1])
    own.start()
    own_slab.start()
    loads = [
        pltpu.make_async_copy(tau.at[t, s], tall.at[s, t], tau_sem.at[t, s]) for t in range(T) for s in range(S)
    ]
    for copy in loads:
        copy.start()
    pl.semaphore_wait(barrier, len(peers) + z + (1 - c) * ((k + LAST) // (LAST + 1)) + (k + 1) // (LAST + 1))

    @pl.when(k == LAST)
    def _():
        tell(wrap_sem, after)

    def remote(src, dst, send, recv, device):
        return pltpu.make_async_remote_copy(
            src_ref=src, dst_ref=dst, send_sem=send, recv_sem=recv,
            device_id=device, device_id_type=pl.DeviceIdType.MESH,
        )

    def rows(g, xx, yy):
        return abig.at[pl.ds(*GROUPS[g]), chunk(xx, yy)]

    def first_rows(g):
        return sink.at[pl.ds(*GROUPS[g])] if g < 2 else rows(g, x, yh)

    def y_copy(g, way):
        device = at(x, yh + STEP[way])
        return remote(first_rows(g), rows(g, x, yh), y_send.at[g, way], y_recv.at[g, way], device)

    def v_copy(g):
        step = STEP[g % 2]
        far = rows(g, x, yh - step)
        return remote(far, far, v_send.at[g], v_recv.at[g], at(x, yh + step))

    def x_copy(g, d, way):
        src = first_rows(g) if d == 0 else rows(g, x, yh + d)
        device = at(x + STEP[way], yh)
        return remote(src, rows(g, x, yh + d), x_send.at[g, d, way], x_recv.at[g, d, way], device)

    def f_copy(g, d):
        step = STEP[d % 2]
        far = rows(g, x - step, yh + d)
        return remote(far, far, f_send.at[g, d], f_recv.at[g, d], at(x + step, yh))

    def guarded(func):
        def call(g, *rest):
            if g == 2:
                pl.when(c == 1)(lambda: func(g, *rest))
            else:
                func(g, *rest)

        return call

    @guarded
    def y_out(g):
        for way in range(2):
            y_copy(g, way).start()

    @guarded
    def x_out(g, d):
        for way in range(2):
            x_copy(g, d, way).start()

    @guarded
    def y_on(g):
        way = g % 2
        for w in (way, 1 - way):
            y_copy(g, w).wait_recv()
            if w == way:
                v_copy(g).start()
            for out_way in range(2):
                x_copy(g, (3, 1)[w], out_way).start()

    @guarded
    def y_end(g):
        v_copy(g).wait_recv()
        for way in range(2):
            x_copy(g, 2, way).start()

    @guarded
    def x_on(g, d):
        x_copy(g, d, d % 2).wait_recv()
        f_copy(g, d).start()

    @guarded
    def arrived(g):
        for d in range(NYH):
            x_copy(g, d, 1 - d % 2).wait_recv()
            f_copy(g, d).wait_recv()

    @guarded
    def all_sent(g):
        v_copy(g).wait_send()
        for way in range(2):
            y_copy(g, way).wait_send()
        for d in range(NYH):
            f_copy(g, d).wait_send()
            for way in range(2):
                x_copy(g, d, way).wait_send()

    def pair(zz):
        return bslab.at[c, pl.ds(2 * lax.rem(zz + NZ, NZ), 2)]

    def along(way, i):
        return z + i if way == 0 else z - i

    def inside(way, i):
        return z + i < NZ if way == 0 else z >= i

    def z_copy(way, i):
        return remote(
            pair(z), pair(z), z_send.at[1 - way, i - 1], z_recv.at[1 - way, i - 1], along_z(i if way == 0 else -i)
        )

    def z_wait(way, i):
        block = pair(along(way, i))
        return remote(block, block, z_send.at[way, i - 1], z_recv.at[way, i - 1], other_core)

    def hand(way, i):
        block = pair(along(way, i))
        return remote(block, block, h_send.at[way, i], h_recv.at[way, i], other_core)

    def down():
        for i in range(1, NZ):

            @pl.when(inside(1, i))
            def _():
                z_copy(1, i).start()

    def up(i):
        @pl.when(inside(0, i))
        def _():
            z_wait(0, i).wait_recv()
            z_copy(0, i).start()
            hand(0, i).start()

    def below(i):
        @pl.when(inside(1, i))
        def _():
            z_wait(1, i).wait_recv()
            hand(1, i).start()

    edges = [remote(tau.at[0, s], tall.at[s, T], e_send.at[s], e_recv.at[s], before) for s in range(S)]
    edge_a = remote(sink.at[0], abig.at[T, mine], e_send.at[S], e_recv.at[S], before)

    loc = remote(slab, bslab.at[c, q], l_send, l_recv, other_y)
    edge_whole = remote(abig.at[0, pl.ds(0, N)], abig.at[T, pl.ds(0, N)], e_send.at[S + 2], e_recv.at[S + 2], other_core)

    @guarded
    def next_rows(g):
        edge_a.wait_recv()
        y_out(g)
        x_out(g, 0)

    y_out(0)
    x_out(0, 0)
    loc.start()

    @pl.when((c == 0) & (k > 0))
    def _():
        edge_a.start()

    y_out(1)
    x_out(1, 0)
    own_slab.wait()
    loc.wait_recv()
    down()
    hand(0, 0).start()
    x_on(0, 0)
    y_on(0)
    next_rows(2)
    x_on(1, 0)
    y_on(1)

    @pl.when(k > 0)
    def _():
        for copy in edges:
            copy.start()

    up(1)
    y_end(0)
    x_on(0, 1)
    x_on(0, 3)
    up(2)
    y_on(2)
    y_end(1)
    up(3)
    x_on(1, 1)
    x_on(1, 3)
    up(4)
    x_on(2, 0)
    x_on(0, 2)
    y_end(2)
    up(5)
    x_on(1, 2)
    up(6)
    up(7)

    @pl.when(k == 0)
    def _():
        pl.semaphore_wait(wrap_sem, 1)
        edge_a.start()
        for copy in edges:
            copy.start()

    for i in range(1, NZ):
        below(i)
    x_on(2, 1)
    x_on(2, 3)
    hand(0, 0).wait_recv()
    for i in range(1, NZ):
        for way in range(2):

            @pl.when(inside(way, i))
            def _():
                hand(way, i).wait_recv()

    for s in range(S):
        for n in range(16):
            parts = [bslab[m, n].astype(F32)[8 * s : 8 * s + 8] for m in range(2)]
            bbig[s, ROWS * n : ROWS * (n + 1)] = jnp.concatenate(parts, axis=0).astype(BF)
        bbig[s, N:] = lower_rows(bbig[s, :N])
    for copy in loads:
        copy.wait()
    for s in range(S):
        u = mm(tall[s, :T].reshape(T * N, W), bbig[s]).astype(BF)
        for t in range(T):
            ubig[s, t, :N] = u[t * N : (t + 1) * N]
            ubig[s, t, N:] = lower_rows(u[t * N : (t + 1) * N])
        if s == 0:
            x_on(2, 2)

    def pairs(t):
        for s in range(S):
            both = mm_nt(tall[s, t : t + 2].reshape(2 * N, W), ubig[s, t])
            vdag[t, s] = both[:N]
            xd = both[N:].astype(BF)
            xbig[t, s, :N] = xd
            xbig[t, s, N:] = lower_rows(xd)

    def fill(t):
        abig[t, N:] = lower_rows(abig[t, :N])

    def trace_d(t):
        for s in range(S):
            dre[t, s], dim[t, s] = trace_adjoint(*halves(abig[t, :N]), *halves(vdag[t, s]))

    def right(t):
        return mm(xbig[t, :, :N].reshape(S * N, W), abig[t])

    def box(t, second):
        for s in range(S):
            first = mm(abig[t + 1, :N], xbig[t, s])
            re, im = trace_adjoint(*halves(first), *halves(second[s * N : (s + 1) * N]))
            out[2, s, t] = re
            out[3, s, t] = -im

    pairs(0)
    pairs(1)
    pairs(2)
    own.wait()
    arrived(0)

    @pl.when(c == 1)
    def _():
        edge_whole.start()

    fill(0)
    fill(1)
    trace_d(0)
    for s in range(S):
        dout[2 * s] = jnp.full((8, 128), dre[0, s], F32)
        dout[2 * s + 1] = jnp.full((8, 128), dim[0, s], F32)
    share = remote(dout, dnext, e_send.at[S + 1], e_recv.at[S + 1], before)
    share.start()
    box(0, right(0))
    trace_d(1)
    for copy in edges:
        copy.wait_recv()
    pairs(3)
    arrived(1)
    fill(2)
    fill(3)
    box(1, right(1))
    box(2, right(2))
    zlast[...] = right(3)
    trace_d(2)
    trace_d(3)
    arrived(2)

    @pl.when(c == 0)
    def _():
        edge_whole.wait_recv()

    box(3, zlast[...])
    share.wait_recv()
    for s in range(S):
        dre[T, s] = jnp.max(dnext[2 * s])
        dim[T, s] = jnp.max(dnext[2 * s + 1])
    for s in range(S):
        for t in range(T):
            ar, ai, br, bi = dre[t, s], dim[t, s], dre[t + 1, s], dim[t + 1, s]
            out[0, s, t] = ar * br + ai * bi
            out[1, s, t] = ai * br - ar * bi
    for g in range(3):
        all_sent(g)
    for copy in edges + [loc, share, hand(0, 0)]:
        copy.wait_send()

    @pl.when(c == 0)
    def _():
        edge_a.wait_send()

    @pl.when(c == 1)
    def _():
        edge_whole.wait_send()

    for i in range(1, NZ):
        for way in range(2):

            @pl.when(inside(way, i))
            def _():
                z_copy(way, i).wait_send()
                hand(way, i).wait_send()


def shards(perambulator, sink_elemental, source_elemental):
    dma = pltpu.SemaphoreType.DMA
    vmem = pltpu.VMEM
    return pl.pallas_call(
        kernel,
        out_shape=jax.ShapeDtypeStruct((4, S, T), F32),
        in_specs=[pl.BlockSpec(memory_space=pl.ANY)] * 3,
        out_specs=pl.BlockSpec(memory_space=pltpu.SMEM),
        scratch_shapes=[
            vmem((S, T + 1, N, W), BF),
            vmem((T + 1, W, W), BF),
            vmem((2, 16, ROWS, W), BF),
            vmem((S, W, W), BF),
            vmem((S, T, W, W), BF),
            vmem((T, S, N, W), F32),
            vmem((T, S, W, W), BF),
            vmem((S * N, W), F32),
            vmem((2 * S, 8, 128), F32),
            vmem((2 * S, 8, 128), F32),
            pltpu.SMEM((T + 1, S), F32),
            pltpu.SMEM((T + 1, S), F32),
            dma((T, S)),
            dma((2,)),
            dma((3, 2)),
            dma((3, 2)),
            dma((3,)),
            dma((3,)),
            dma((3, NYH, 2)),
            dma((3, NYH, 2)),
            dma((3, NYH)),
            dma((3, NYH)),
            dma,
            dma,
            dma((2, NZ - 1)),
            dma((2, NZ - 1)),
            dma((2, NZ)),
            dma((2, NZ)),
            dma((S + 3,)),
            dma((S + 3,)),
            pltpu.SemaphoreType.REGULAR,
        ],
        compiler_params=pltpu.CompilerParams(
            collective_id=0, has_side_effects=True, vmem_limit_bytes=60 * 1024 * 1024
        ),
        cost_estimate=pl.CostEstimate(flops=5_400_000_000, bytes_accessed=2_300_000, transcendentals=0),
    )(perambulator, sink_elemental, source_elemental.reshape(ROWS, W))


def solution(mesh):
    in_specs = (P("snk", "src", None, None), P("snk", "src", None), P("src", "snk", None))
    out_specs = P(None, "src", "snk")
    return jax.shard_map(shards, mesh=mesh, in_specs=in_specs, out_specs=out_specs, check_vma=False)
```
